256 devices in a mesh: section: 8 (over y, z_hi), expert: 32 (over x, z_lo, core).
Axes of the slice: x: 4, y: 4, z: 8 (z_hi: 2, z_lo: 4; z = z_hi * 4 + z_lo), core: 2. Of those that a mesh axis runs over, the one named last changes fastest.
Arguments:
- act_fwd: bfloat16 [8, 4096, 4096], P('section', 'expert'), may hold values from -6 to 6
- act_rev: bfloat16 [8, 4096, 4096], P('section', 'expert'), may hold values from -6 to 6
- ids_fwd: int32 [8, 4096, 2], P('section', 'expert'), may hold values from 0 to 15, all different within a row; in each aligned block of 128 rows (0 to 127, 128 to 255, ..., all dimensions but the last counted through in order) at most 24 rows name the same one
- ids_rev: int32 [8, 4096, 2], P('section', 'expert'), may hold values from 0 to 15, all different within a row; in each aligned block of 128 rows (0 to 127, 128 to 255, ..., all dimensions but the last counted through in order) at most 24 rows name the same one
- probs_fwd: float32 [8, 4096, 2], P('section', 'expert'), may hold values from 0.05 to 1
- probs_rev: float32 [8, 4096, 2], P('section', 'expert'), may hold values from 0.05 to 1
- w_gate: bfloat16 [8, 4096, 12288], P('section', None, 'expert'), may hold values from -0.09375 to 0.09375
- w_up: bfloat16 [8, 4096, 12288], P('section', None, 'expert'), may hold values from -0.09375 to 0.09375
- w_down: bfloat16 [8, 12288, 4096], P('section', 'expert'), may hold values from -0.21875 to 0.21875
Outputs:
- out_fwd: bfloat16 [8, 4096, 4096], P('section', 'expert')
- out_rev: bfloat16 [8, 4096, 4096], P('section', 'expert')
The draws below stay inside these ranges and needn't reach their ends.
Inputs may be any that keep to these rules, and one draw needn't show every extreme that they name: `ids_fwd`: each row names 2 different experts. Within the 128 rows of one device (aligned blocks) no expert is named by more than 24 rows, and some block reaches 24. `ids_rev`: as for ids_fwd.
All inputs are finite; a program needn't handle non-finite values.
Results may differ from the reference program's by a relative error of at most 0.0048.
Values may be sent and summed in bfloat16 or wider, within the bound.
No kernel may reach another device: no remote copies, remote signals or barrier semaphores. Data moves between devices by JAX's collectives and lax.ppermute only.
A program may use at most 128 MiB of HBM per device.

```python
import math
import jax
import jax.numpy as jnp
import numpy as np
from jax import lax

D = 4096
HID = 768
TOPK = 2
TOK = 128
HALF = 384
SECTIONS = 8
EXPERTS = 16
TOKENS = 4096
CAP = 24
N_EXPERT = 32


def levels(key, shape, cuts, smallest, largest):
    def one(dim, blocks):
        steps = jax.random.uniform(jax.random.fold_in(jax.random.fold_in(key, 6), dim), (blocks,), jnp.float32, smallest / len(cuts), largest / len(cuts))
        return jnp.repeat(jnp.exp(steps), shape[dim] // blocks).reshape((-1,) + (1,) * (len(shape) - dim - 1))

    level = one(*cuts[0])
    for cut in cuts[1:]:
        level = level * one(*cut)
    return level


def deal_out(stream_key, own, number, rows, count, top, most, slope):
    sequence = jax.random.permutation(stream_key, count)
    crowded, ordinary = shares(count, rows * top, most, slope, True), shares(count, rows * top, most, slope, False)
    places = jnp.arange(count)

    def named(lengths, turn):
        used = int((lengths > 0).sum())
        fixed = max(1, used // 4)
        passed = fixed + (places - fixed + turn * (used - fixed)) % max(1, count - fixed)
        return jnp.zeros((count,), jnp.int32).at[sequence[jnp.where(places < fixed, places, passed)]].set(jnp.asarray(lengths, jnp.int32))

    lengths = jnp.where(number % 4 == 0, named(crowded, number // 4), named(ordinary, number - number // 4 - 1))
    mixed = jax.random.permutation(jax.random.fold_in(own, 3), count)
    donor, taker = mixed[0:count // 2 * 2:2], mixed[1:count // 2 * 2:2]
    slack = jnp.minimum(lengths[donor] - 1, most - lengths[taker]) // 2
    slack = jnp.where((donor == sequence[0]) | (taker == sequence[0]) | (lengths[taker] == 0), 0, jnp.maximum(slack, 0))
    passed = jax.random.randint(jax.random.fold_in(own, 4), (count // 2,), 0, 1 << 20) % (slack + 1)
    lengths = lengths.at[donor].add(-passed).at[taker].add(passed)
    members = jnp.searchsorted(jnp.cumsum(lengths), jnp.arange(rows * top), side="right").astype(jnp.int32)
    grid = members.reshape(top, rows).T
    grid = grid[jax.random.permutation(jax.random.fold_in(own, 1), rows)]
    turn = jax.random.randint(jax.random.fold_in(own, 2), (rows, 1), 0, top)
    return jnp.take_along_axis(grid, (jnp.arange(top)[None, :] + turn) % top, axis=1)


def shares(count, total, bound, skew, full):
    weights = [(1 << 20) // math.isqrt(rank ** skew) + 1 for rank in range(1, count + 1)]
    largest = bound if full else min(bound, max(-(-total // count), total * weights[0] // sum(weights)))
    least = 1 if total - largest >= count - 1 else 0
    given, spare = [largest] + [least] * (count - 1), total - largest - least * (count - 1)
    while spare > 0:
        free = [i for i in range(1, count) if given[i] < largest] or [i for i in range(1, count) if given[i] < bound]
        pool, left = sum([weights[i] for i in free]), spare
        for i in free:
            more = min(bound - given[i], max(1, left * weights[i] // pool), spare)
            given[i] = given[i] + more
            spare = spare - more
    return np.array(given)


def noise(rng, dims, scale, reach, split=(), kind=jnp.bfloat16):
    drawn = scale * jax.random.normal(rng, dims, jnp.float32)
    if split:
        drawn = drawn * levels(rng, dims, split, -0.22, 0.18)
    return jnp.clip(drawn, -reach, reach).astype(kind)


def setup_inputs(seed: int = 0) -> dict:
    key_list = jax.random.split(jax.random.key(seed), 10)
    act_fwd = noise(key_list[0], (SECTIONS, TOKENS, D), 1.0, 6.0, ((0, 8), (1, 32)))
    act_rev = noise(key_list[1], (SECTIONS, TOKENS, D), 1.0, 6.0, ((0, 8), (1, 32)))
    ids_fwd_keys = jax.random.split(jax.random.fold_in(key_list[2], 1), SECTIONS * TOKENS // TOK)
    ids_fwd_turns = jax.random.permutation(jax.random.fold_in(key_list[2], 3), SECTIONS * TOKENS // TOK)
    ids_fwd = jax.vmap(lambda own, number: deal_out(jax.random.fold_in(key_list[2], 2), own, number, TOK, EXPERTS, TOPK, CAP, 2))(ids_fwd_keys, ids_fwd_turns).reshape((SECTIONS, TOKENS, TOPK))
    ids_rev_keys = jax.random.split(jax.random.fold_in(key_list[3], 1), SECTIONS * TOKENS // TOK)
    ids_rev_turns = jax.random.permutation(jax.random.fold_in(key_list[3], 3), SECTIONS * TOKENS // TOK)
    ids_rev = jax.vmap(lambda own, number: deal_out(jax.random.fold_in(key_list[3], 2), own, number, TOK, EXPERTS, TOPK, CAP, 2))(ids_rev_keys, ids_rev_turns).reshape((SECTIONS, TOKENS, TOPK))
    probs_fwd = jnp.clip(jnp.exp(math.log(1.0) - 2.9957323 * jax.random.uniform(key_list[4], (SECTIONS, TOKENS, TOPK), jnp.float32) ** levels(key_list[4], (SECTIONS, TOKENS, TOPK), ((0, 8), (1, 32)), -0.2, 0.2)), 0.05, 1.0)
    probs_rev = jnp.clip(jnp.exp(math.log(1.0) - 2.9957323 * jax.random.uniform(key_list[5], (SECTIONS, TOKENS, TOPK), jnp.float32) ** levels(key_list[5], (SECTIONS, TOKENS, TOPK), ((0, 8), (1, 32)), -0.2, 0.2)), 0.05, 1.0)
    w_gate = noise(key_list[6], (SECTIONS, D, EXPERTS * HID), D ** -0.5, 0.09375, ((0, 8), (2, 32)))
    w_up = noise(key_list[7], (SECTIONS, D, EXPERTS * HID), D ** -0.5, 0.09375, ((0, 8), (2, 32)))
    w_down = noise(key_list[8], (SECTIONS, EXPERTS * HID, D), HID ** -0.5, 0.21875, ((0, 8), (1, 32)))
    return dict(act_fwd=act_fwd, act_rev=act_rev, ids_fwd=ids_fwd, ids_rev=ids_rev, probs_fwd=probs_fwd, probs_rev=probs_rev, w_gate=w_gate, w_up=w_up, w_down=w_down)


def expert_apply(chosen, w_gate_s, w_up_s, w_down_s, expert_id):
    pieces = []
    for half_id in range(2):
        start = (expert_id * HID + half_id * HALF).astype(jnp.int32)
        gate_cols = lax.dynamic_slice_in_dim(w_gate_s, start, HALF, 1)
        up_cols = lax.dynamic_slice_in_dim(w_up_s, start, HALF, 1)
        down_rows = lax.dynamic_slice_in_dim(w_down_s, start, HALF, 0)
        gate_pre = jnp.dot(chosen, gate_cols, preferred_element_type=jnp.float32)
        up_pre = jnp.dot(chosen, up_cols, preferred_element_type=jnp.float32)
        hidden = (jax.nn.silu(gate_pre) * up_pre).astype(jnp.bfloat16)
        partial_value = jnp.dot(hidden, down_rows, preferred_element_type=jnp.float32).astype(jnp.bfloat16)
        pieces.append(partial_value.astype(jnp.float32))
    return (pieces[0] + pieces[1]).astype(jnp.bfloat16)


def moe_layer(tokens_in, route_ids, probs, w_gate_s, w_up_s, w_down_s):
    route_total = TOKENS * TOPK
    slot_total = N_EXPERT * CAP
    flat_ids = route_ids.reshape(-1).astype(jnp.int32)
    weights = probs / jnp.sum(probs, axis=1, keepdims=True)

    def one_expert(accumulated, expert_id):
        is_this = flat_ids == expert_id
        rank_in = jnp.cumsum(is_this.astype(jnp.int32)) - 1
        placed_at = jnp.where(is_this, rank_in, slot_total).astype(jnp.int32)
        slot_index = jnp.zeros((slot_total,), jnp.int32).at[placed_at].set(jnp.arange(route_total, dtype=jnp.int32), mode="drop")
        slot_used = jnp.zeros((slot_total,), jnp.float32).at[placed_at].set(1.0, mode="drop")
        chosen = tokens_in[slot_index // TOPK]
        result = expert_apply(chosen, w_gate_s, w_up_s, w_down_s, expert_id).astype(jnp.float32)
        accumulated = accumulated.at[slot_index].add(result * slot_used[:, None])
        return accumulated, None

    start_sum = jnp.zeros((route_total, D), jnp.float32)
    accumulated, unused = lax.scan(one_expert, start_sum, jnp.arange(EXPERTS, dtype=jnp.int32))
    per_route = accumulated.reshape(TOKENS, TOPK, D)
    mixed = tokens_in.astype(jnp.float32) + jnp.sum(per_route * weights[:, :, None], axis=1)
    return mixed.astype(jnp.bfloat16)


def reference(act_fwd, act_rev, ids_fwd, ids_rev, probs_fwd, probs_rev, w_gate, w_up, w_down):
    arrived_fwd = jnp.roll(act_fwd, 1, axis=0)
    arrived_rev = jnp.roll(act_rev, -1, axis=0)
    forward_list = []
    reverse_list = []
    for section_id in range(SECTIONS):
        forward_list.append(moe_layer(arrived_fwd[section_id], ids_fwd[section_id], probs_fwd[section_id], w_gate[section_id], w_up[section_id], w_down[section_id]))
        reverse_list.append(moe_layer(arrived_rev[section_id], ids_rev[section_id], probs_rev[section_id], w_gate[section_id], w_up[section_id], w_down[section_id]))
    return (jnp.stack(forward_list), jnp.stack(reverse_list))
```

```python
import jax
import jax.numpy as jnp
from jax import lax
from jax.sharding import Mesh
from jax.sharding import PartitionSpec as P

EXPERTS = 16
CAP = 24
X, Z, Y = 4, 4, 4
BF = jnp.bfloat16
F32 = jnp.float32


def slots_of(ids):
    flat = ids.reshape(-1)
    n = flat.shape[0]
    one_hot = (flat[:, None] == jnp.arange(EXPERTS, dtype=jnp.int32)[None, :]).astype(BF)
    place = jnp.arange(n, dtype=jnp.int32)
    below = (place[:, None] > place[None, :]).astype(BF)
    counts = jnp.dot(below, one_hot, preferred_element_type=F32)
    rank = jnp.sum(counts * one_hot.astype(F32), axis=1).astype(jnp.int32)
    return (flat * CAP + rank).reshape(ids.shape)


def outgoing(tokens, slots, z_lo):
    t = slots.shape[1]
    row = jnp.arange(X * Z * CAP, dtype=jnp.int32)
    to_x, source, rank = row // (Z * CAP), row // CAP % Z, row % CAP
    target = (to_x * Z + z_lo) * CAP + rank
    held = jnp.arange(Z * t, dtype=jnp.int32) // t
    flat = slots.reshape(Z * t, 2)
    hit = (flat[None, :, 0] == target[:, None]) | (flat[None, :, 1] == target[:, None])
    pick = (hit & (held[None, :] == source[:, None])).astype(BF)
    return jnp.dot(pick, tokens, preferred_element_type=F32).astype(BF)


def expert(rows, w_gate, w_up, w_down):
    gate = jnp.dot(rows, w_gate, preferred_element_type=F32)
    up = jnp.dot(rows, w_up, preferred_element_type=F32)
    hidden = (jax.nn.silu(gate) * up).astype(BF)
    return jnp.dot(hidden, w_down, preferred_element_type=F32).astype(BF)


def combine(home, back, slots, probs):
    gates = probs / jnp.sum(probs, axis=1, keepdims=True)
    place = jnp.arange(EXPERTS * CAP, dtype=jnp.int32)
    mix = jnp.sum(
        jnp.where(slots[:, :, None] == place[None, None, :], gates[:, :, None], 0.0), axis=1
    )
    high = lax.reduce_precision(mix, 8, 7)
    both = jnp.concatenate([high, mix - high], axis=0).astype(BF)
    summed = jnp.dot(both, back, preferred_element_type=F32)
    t = home.shape[0]
    return (home.astype(F32) + (summed[:t] + summed[t:])).astype(BF)


def after(value, *others):
    return lax.optimization_barrier((value, *others))[0]


def body(act_fwd, act_rev, ids_fwd, ids_rev, probs_fwd, probs_rev, w_gate, w_up, w_down):
    z_hi, z_lo = lax.axis_index("z_hi"), lax.axis_index("z_lo")
    upper = z_hi == 1
    act_fwd, act_rev = act_fwd[0], act_rev[0]
    t, d = act_fwd.shape

    def choose(a, b):
        return jnp.where(upper, a, b)

    first = choose(act_rev, act_fwd)
    hop = [((y - 1) % Y * 2 + 1, y * 2 + 1) for y in range(Y)]
    hop += [((y + 1) % Y * 2, y * 2) for y in range(Y)]
    second = lax.ppermute(choose(act_fwd, act_rev), ("y", "z_hi"), hop)

    def ring(block):
        full = lax.all_gather(block, ("z_hi", "z_lo"), axis=0, tiled=True)
        return full

    def arrived(full):
        return lax.dynamic_slice_in_dim(full, (1 - z_hi) * Z * t, Z * t, 0)

    def at_home(full):
        return lax.dynamic_slice_in_dim(full, ((1 - z_hi) * Z + z_lo) * t, t, 0)

    full_1 = ring(first)

    ids = [choose(ids_fwd[0], ids_rev[0]), choose(ids_rev[0], ids_fwd[0])]
    probs = [choose(probs_fwd[0], probs_rev[0]), choose(probs_rev[0], probs_fwd[0])]
    slots = [slots_of(i) for i in ids]
    slots_all = lax.all_gather(jnp.stack(slots), "z_lo", axis=0)

    swap = [(0, 1), (1, 0)]
    gate_w = jnp.concatenate([w_gate[0], lax.ppermute(w_gate[0], "core", swap)], axis=1)
    up_w = jnp.concatenate([w_up[0], lax.ppermute(w_up[0], "core", swap)], axis=1)
    down_w = jnp.concatenate([w_down[0], lax.ppermute(w_down[0], "core", swap)], axis=0)

    full_2 = ring(after(second, full_1))

    outs = []
    for p, full in enumerate((full_1, full_2)):
        sent = outgoing(arrived(full), slots_all[:, p], z_lo)
        rows = lax.all_to_all(sent, "x", split_axis=0, concat_axis=0, tiled=True)
        done = expert(rows, gate_w, up_w, down_w)
        back = lax.all_to_all(done, ("x", "z_lo"), split_axis=0, concat_axis=0, tiled=True)
        outs.append(combine(at_home(full), back, slots[p], probs[p]))

    return (choose(outs[0], outs[1])[None], choose(outs[1], outs[0])[None])


def solution(mesh):
    split = Mesh(mesh.devices.reshape(Y, 2, X, Z, 2), ("y", "z_hi", "x", "z_lo", "core"))
    section, spread = ("y", "z_hi"), ("x", "z_lo", "core")
    tokens = P(section, spread, None)
    return jax.shard_map(
        body,
        mesh=split,
        in_specs=(tokens,) * 6 + (P(section, None, spread),) * 2 + (tokens,),
        out_specs=(tokens, tokens),
        check_vma=False,
    )
```

```python
import jax
import jax.numpy as jnp
from jax import lax
from jax.experimental import pallas as pl
from jax.experimental.pallas import tpu as pltpu
from jax.sharding import Mesh
from jax.sharding import PartitionSpec as P

EXPERTS = 16
CAP = 24
X, Z, Y = 4, 4, 4
BF = jnp.bfloat16
F32 = jnp.float32


def slots_of(ids):
    flat = ids.reshape(-1)
    n = flat.shape[0]
    one_hot = (flat[:, None] == jnp.arange(EXPERTS, dtype=jnp.int32)[None, :]).astype(BF)
    place = jnp.arange(n, dtype=jnp.int32)
    below = (place[:, None] > place[None, :]).astype(BF)
    counts = jnp.dot(below, one_hot, preferred_element_type=F32)
    rank = jnp.sum(counts * one_hot.astype(F32), axis=1).astype(jnp.int32)
    return (flat * CAP + rank).reshape(ids.shape)


def outgoing(parts, slots, sources, turn, z_lo):
    t, n = parts[0].shape[0], len(parts)
    row = jnp.arange(X * n * CAP, dtype=jnp.int32)
    block, which, rank = row // (n * CAP), row // CAP % n, row % CAP
    target = ((turn + block) % X * Z + z_lo) * CAP + rank
    held = jnp.arange(n * t, dtype=jnp.int32) // t
    flat = jnp.concatenate([lax.dynamic_index_in_dim(slots, (z_lo - s) % Z, 0, False) for s in sources], axis=0)
    hit = (flat[None, :, 0] == target[:, None]) | (flat[None, :, 1] == target[:, None])
    pick = (hit & (held[None, :] == which[:, None])).astype(BF)
    return jnp.dot(pick, jnp.concatenate(parts, axis=0), preferred_element_type=F32).astype(BF)


def over_x(sent):
    n = sent.shape[0] // X
    blocks = [sent[i * n : (i + 1) * n] for i in range(X)]
    moved = [lax.ppermute(blocks[i], "x", [(j, (j + i) % X) for j in range(X)]) for i in range(1, X)]
    return [blocks[0], *moved]


def place(from_x, source, rank):
    return (from_x * Z + source) * CAP + rank


def to_matrix(to):
    row = jnp.arange(to.shape[0], dtype=jnp.int32)
    return (row[:, None] == to[None, :]).astype(BF)


STEPS = 4


def expert_kernel(n_parts, *refs):
    parts, (order, g0, g1, u0, u1, d0, d1, out, gate, up, hidden) = refs[:n_parts], refs[n_parts:]
    step = pl.program_id(0)

    @pl.when(step == 0)
    def _():
        gate[...] = jnp.zeros_like(gate)
        up[...] = jnp.zeros_like(up)

    @pl.when(step < STEPS)
    def _():
        rows = jnp.concatenate([p[...] for p in parts], axis=0)
        gate[...] += jnp.dot(rows, jnp.concatenate([g0[...], g1[...]], axis=1), preferred_element_type=F32)
        up[...] += jnp.dot(rows, jnp.concatenate([u0[...], u1[...]], axis=1), preferred_element_type=F32)

    @pl.when(step == STEPS - 1)
    def _():
        pre = gate[...]
        value = (pre / (1.0 + jnp.exp(-pre)) * up[...]).astype(BF)
        hidden[...] = jnp.dot(order[...], value, preferred_element_type=F32).astype(BF)

    @pl.when(step >= STEPS)
    def _():
        down = jnp.concatenate([d0[...], d1[...]], axis=0)
        out[...] = jnp.dot(hidden[...], down, preferred_element_type=F32).astype(BF)


def expert(parts, order, gates, ups, downs, flops):
    n, d = order.shape[0], parts[0].shape[1]
    half = gates[0].shape[1]
    cols = d // STEPS

    def first(i):
        return jnp.minimum(i, STEPS - 1)

    def second(i):
        return jnp.maximum(i - STEPS, 0)

    in_specs = [pl.BlockSpec((p.shape[0], cols), lambda i: (0, first(i))) for p in parts]
    in_specs += [pl.BlockSpec((n, n), lambda i: (0, 0))]
    in_specs += [pl.BlockSpec((cols, half), lambda i: (first(i), 0))] * 4
    in_specs += [pl.BlockSpec((half, cols), lambda i: (0, second(i)))] * 2
    return pl.pallas_call(
        lambda *refs: expert_kernel(len(parts), *refs),
        grid=(2 * STEPS,),
        in_specs=in_specs,
        out_specs=pl.BlockSpec((n, cols), lambda i: (0, second(i))),
        out_shape=jax.ShapeDtypeStruct((n, d), BF),
        scratch_shapes=[
            pltpu.VMEM((n, 2 * half), F32),
            pltpu.VMEM((n, 2 * half), F32),
            pltpu.VMEM((n, 2 * half), BF),
        ],
        compiler_params=pltpu.CompilerParams(vmem_limit_bytes=40 * 2**20),
        cost_estimate=pl.CostEstimate(flops=flops, bytes_accessed=10**6, transcendentals=0),
        name="expert",
    )(*parts, order, *gates, *ups, *downs)


def mixing(slots, probs):
    gates = probs / jnp.sum(probs, axis=1, keepdims=True)
    spot = jnp.arange(EXPERTS * CAP, dtype=jnp.int32)
    mix = jnp.sum(
        jnp.where(slots[:, :, None] == spot[None, None, :], gates[:, :, None], 0.0), axis=1
    )
    high = lax.reduce_precision(mix, 8, 7)
    return jnp.concatenate([high, mix - high], axis=0).astype(BF)


def combine(home, back, mix):
    summed = jnp.dot(mix, back, preferred_element_type=F32)
    t = home.shape[0]
    return (home.astype(F32) + (summed[:t] + summed[t:])).astype(BF)


def finish_kernel(upper, home, back, mix, other, out_a, out_b):
    last = combine(home[...], back[...], mix[...])
    swap = upper[0] == 1
    out_a[...] = jnp.where(swap, other[...], last)
    out_b[...] = jnp.where(swap, last, other[...])


def finish(upper, home, back, mix, other):
    t, d = home.shape
    cols = 1024

    def tall(rows):
        return pl.BlockSpec((rows, cols), lambda i: (0, i))

    return pl.pallas_call(
        finish_kernel,
        grid=(d // cols,),
        in_specs=[
            pl.BlockSpec(memory_space=pltpu.SMEM),
            tall(t),
            tall(back.shape[0]),
            pl.BlockSpec(mix.shape, lambda i: (0, 0)),
            tall(t),
        ],
        out_specs=[tall(t), tall(t)],
        out_shape=[jax.ShapeDtypeStruct((t, d), BF)] * 2,
        compiler_params=pltpu.CompilerParams(vmem_limit_bytes=40 * 2**20),
        name="finish",
    )(upper.astype(jnp.int32)[None], home, back, mix, other)


def after(value, *others):
    return lax.optimization_barrier((value, *others))[0]


def shift_ring(block, by):
    n = 2 * Z
    return lax.ppermute(block, ("z_hi", "z_lo"), [(i, (i + by) % n) for i in range(n)])


def body(act_fwd, act_rev, ids_fwd, ids_rev, probs_fwd, probs_rev, w_gate, w_up, w_down):
    x, z_hi, z_lo = lax.axis_index("x"), lax.axis_index("z_hi"), lax.axis_index("z_lo")
    upper = z_hi == 1
    act_fwd, act_rev = act_fwd[0], act_rev[0]

    def choose(a, b):
        return jnp.where(upper, a, b)

    first = choose(act_rev, act_fwd)
    hop = [((y - 1) % Y * 2 + 1, y * 2 + 1) for y in range(Y)]
    hop += [((y + 1) % Y * 2, y * 2) for y in range(Y)]
    second = lax.ppermute(choose(act_fwd, act_rev), ("y", "z_hi"), hop)

    ids = [choose(ids_fwd[0], ids_rev[0]), choose(ids_rev[0], ids_fwd[0])]
    probs = [choose(probs_fwd[0], probs_rev[0]), choose(probs_rev[0], probs_fwd[0])]
    slots = [slots_of(i) for i in ids]
    mine = jnp.stack(slots)
    slots_all = jnp.stack(
        [mine]
        + [lax.ppermute(mine, "z_lo", [(j, (j + i) % Z) for j in range(Z)]) for i in range(1, Z)]
    )

    swap = [(0, 1), (1, 0)]
    gates, ups, downs = ((w[0], lax.ppermute(w[0], "core", swap)) for w in (w_gate, w_up, w_down))

    low = z_lo < 2
    edge = (z_lo == 0) | (z_lo == Z - 1)
    sources = (
        jnp.where(low, 3, 0),
        jnp.where(low, 2, 1),
        jnp.where(low, 0, 3),
        jnp.where(low, 1, 2),
    )
    row = jnp.arange(X * Z * CAP, dtype=jnp.int32)
    group_of, by_x, far, rank = row // (X * 2 * CAP), row // (2 * CAP) % X, row // CAP % 2, row % CAP
    near_far = [jnp.where(far == 0, sources[i], sources[i + 1]) for i in (0, 2)]
    source = jnp.where(group_of == 0, *near_far)
    order_1 = to_matrix(place(by_x, source, rank))
    by_shift, which = row // (Z * CAP), row // CAP % Z
    source = jnp.where(
        which < 2,
        jnp.where(which == 0, sources[0], sources[1]),
        jnp.where(which == 2, sources[2], sources[3]),
    )
    order_2 = to_matrix(place((x - by_shift) % X, source, rank))
    mixes = [mixing(slots[p], probs[p]) for p in range(2)]
    up, down = [first], [first]

    def at(p, same, k):
        a, b = (up, down) if same else (down, up)
        k = [i + 2 * p for i in k]
        return jnp.where(
            low, jnp.where(edge, a[k[0]], a[k[1]]), jnp.where(edge, b[k[0]], b[k[1]])
        )

    def group(p, same):
        if same:
            return [at(p, True, (1, 2)), at(p, True, (2, 3))]
        return [at(p, False, (4, 3)), at(p, False, (5, 4))]

    def all_x(sent):
        return lax.all_to_all(
            sent.reshape(X, -1, sent.shape[1]), "x", split_axis=0, concat_axis=0, tiled=True
        ).reshape(sent.shape)

    def back(done):
        return lax.all_to_all(
            done.reshape(EXPERTS, CAP, -1), ("x", "z_lo"), split_axis=0, concat_axis=0, tiled=True
        ).reshape(done.shape)

    def home(p):
        return jnp.where(low, down[4 + 2 * p], up[4 + 2 * p])

    def hops(step, *beside):
        above, below = up[-1], down[-1]
        if step == 3:
            above, below = jnp.where(low, above, second), jnp.where(low, second, below)
        ends = (shift_ring(above, 1), shift_ring(below, -1))
        ends, beside = lax.optimization_barrier((ends, beside))
        up.append(ends[0])
        down.append(ends[1])
        return beside

    def picked(parts, p, froms, turn):
        return outgoing(parts, slots_all[:, p], froms, turn, z_lo)

    (gates,) = hops(1, gates)
    ups, slots_all = hops(2, ups, slots_all)
    downs, mixes = hops(3, downs, mixes)
    sent_a = picked(group(0, True), 0, sources[:2], 0)
    hops(4, sent_a)
    got_a = all_x(sent_a)
    order_1, order_2 = hops(5, got_a, order_1, order_2)[1:]
    sent_b = picked(group(0, False), 0, sources[2:], 0)
    gates = hops(6, sent_b, gates)[1]
    done_1 = expert([got_a, all_x(sent_b)], order_1, gates, ups, downs, 10**8)
    hops(7, done_1)
    back_1 = back(done_1)
    got_2 = over_x(picked(group(1, True) + group(1, False), 1, sources, x))
    done_2 = expert(got_2, order_2, gates, ups, downs, 2 * 10**11)
    out_1 = combine(home(0), after(back_1, done_2), mixes[0])
    out_a, out_b = finish(upper, home(1), back(done_2), mixes[1], out_1)
    return out_a[None], out_b[None]


def solution(mesh):
    split = Mesh(mesh.devices.reshape(Y, 2, X, Z, 2), ("y", "z_hi", "x", "z_lo", "core"))
    section, spread = ("y", "z_hi"), ("x", "z_lo", "core")
    tokens = P(section, spread, None)
    return jax.shard_map(
        body,
        mesh=split,
        in_specs=(tokens,) * 6 + (P(section, None, spread),) * 2 + (tokens,),
        out_specs=(tokens, tokens),
        check_vma=False,
    )
```

```python
import jax
import jax.numpy as jnp
from jax import lax
from jax.experimental import pallas as pl
from jax.experimental.pallas import tpu as pltpu
from jax.sharding import Mesh
from jax.sharding import PartitionSpec as P

EXPERTS = 16
CAP = 24
X, Z, Y = 4, 4, 4
BF = jnp.bfloat16
F32 = jnp.float32


def slots_of(ids):
    flat = ids.reshape(-1)
    n = flat.shape[0]
    one_hot = (flat[:, None] == jnp.arange(EXPERTS, dtype=jnp.int32)[None, :]).astype(BF)
    place = jnp.arange(n, dtype=jnp.int32)
    below = (place[:, None] > place[None, :]).astype(BF)
    counts = jnp.dot(below, one_hot, preferred_element_type=F32)
    rank = jnp.sum(counts * one_hot.astype(F32), axis=1).astype(jnp.int32)
    return (flat * CAP + rank).reshape(ids.shape)


def outgoing(parts, slots, sources, turn, z_lo):
    t, n = parts[0].shape[0], len(parts)
    row = jnp.arange(X * n * CAP, dtype=jnp.int32)
    block, which, rank = row // (n * CAP), row // CAP % n, row % CAP
    target = ((turn + block) % X * Z + z_lo) * CAP + rank
    held = jnp.arange(n * t, dtype=jnp.int32) // t
    flat = jnp.concatenate([lax.dynamic_index_in_dim(slots, (z_lo - s) % Z, 0, False) for s in sources], axis=0)
    hit = (flat[None, :, 0] == target[:, None]) | (flat[None, :, 1] == target[:, None])
    pick = (hit & (held[None, :] == which[:, None])).astype(BF)
    return jnp.dot(pick, jnp.concatenate(parts, axis=0), preferred_element_type=F32).astype(BF)


def over_x(sent):
    n = sent.shape[0] // X
    blocks = [sent[i * n : (i + 1) * n] for i in range(X)]
    moved = [lax.ppermute(blocks[i], "x", [(j, (j + i) % X) for j in range(X)]) for i in range(1, X)]
    return [blocks[0], *moved]


def place(from_x, source, rank):
    return (from_x * Z + source) * CAP + rank


def to_matrix(to):
    row = jnp.arange(to.shape[0], dtype=jnp.int32)
    return (row[:, None] == to[None, :]).astype(BF)


STEPS = 4


def expert_kernel(n_parts, *refs):
    parts, (order, g0, g1, u0, u1, d0, d1, out, gate, up, hidden) = refs[:n_parts], refs[n_parts:]
    step = pl.program_id(0)

    @pl.when(step == 0)
    def _():
        gate[...] = jnp.zeros_like(gate)
        up[...] = jnp.zeros_like(up)

    @pl.when(step < STEPS)
    def _():
        rows = jnp.concatenate([p[...] for p in parts], axis=0)
        gate[...] += jnp.dot(rows, jnp.concatenate([g0[...], g1[...]], axis=1), preferred_element_type=F32)
        up[...] += jnp.dot(rows, jnp.concatenate([u0[...], u1[...]], axis=1), preferred_element_type=F32)

    @pl.when(step == STEPS - 1)
    def _():
        pre = gate[...]
        value = (pre / (1.0 + jnp.exp(-pre)) * up[...]).astype(BF)
        hidden[...] = jnp.dot(order[...], value, preferred_element_type=F32).astype(BF)

    @pl.when(step >= STEPS)
    def _():
        down = jnp.concatenate([d0[...], d1[...]], axis=0)
        out[...] = jnp.dot(hidden[...], down, preferred_element_type=F32).astype(BF)


def expert(parts, order, gates, ups, downs, flops):
    n, d = order.shape[0], parts[0].shape[1]
    half = gates[0].shape[1]
    cols = d // STEPS

    def first(i):
        return jnp.minimum(i, STEPS - 1)

    def second(i):
        return jnp.maximum(i - STEPS, 0)

    in_specs = [pl.BlockSpec((p.shape[0], cols), lambda i: (0, first(i))) for p in parts]
    in_specs += [pl.BlockSpec((n, n), lambda i: (0, 0))]
    in_specs += [pl.BlockSpec((cols, half), lambda i: (first(i), 0))] * 4
    in_specs += [pl.BlockSpec((half, cols), lambda i: (0, second(i)))] * 2
    return pl.pallas_call(
        lambda *refs: expert_kernel(len(parts), *refs),
        grid=(2 * STEPS,),
        in_specs=in_specs,
        out_specs=pl.BlockSpec((n, cols), lambda i: (0, second(i))),
        out_shape=jax.ShapeDtypeStruct((n, d), BF),
        scratch_shapes=[
            pltpu.VMEM((n, 2 * half), F32),
            pltpu.VMEM((n, 2 * half), F32),
            pltpu.VMEM((n, 2 * half), BF),
        ],
        compiler_params=pltpu.CompilerParams(vmem_limit_bytes=58 * 2**20),
        cost_estimate=pl.CostEstimate(flops=flops, bytes_accessed=10**6, transcendentals=0),
        name="expert",
    )(*parts, order, *gates, *ups, *downs)


def mixing(slots, probs):
    gates = probs / jnp.sum(probs, axis=1, keepdims=True)
    spot = jnp.arange(EXPERTS * CAP, dtype=jnp.int32)
    mix = jnp.sum(
        jnp.where(slots[:, :, None] == spot[None, None, :], gates[:, :, None], 0.0), axis=1
    )
    high = lax.reduce_precision(mix, 8, 7)
    return jnp.concatenate([high, mix - high], axis=0).astype(BF)


def combine(home, back, mix):
    summed = jnp.dot(mix, back, preferred_element_type=F32)
    t = home.shape[0]
    return (home.astype(F32) + (summed[:t] + summed[t:])).astype(BF)


def finish_kernel(upper, home, back, mix, other, out_a, out_b):
    last = combine(home[...], back[...], mix[...])
    swap = upper[0] == 1
    out_a[...] = jnp.where(swap, other[...], last)
    out_b[...] = jnp.where(swap, last, other[...])


def finish(upper, home, back, mix, other):
    t, d = home.shape
    cols = 1024

    def tall(rows):
        return pl.BlockSpec((rows, cols), lambda i: (0, i))

    return pl.pallas_call(
        finish_kernel,
        grid=(d // cols,),
        in_specs=[
            pl.BlockSpec(memory_space=pltpu.SMEM),
            tall(t),
            tall(back.shape[0]),
            pl.BlockSpec(mix.shape, lambda i: (0, 0)),
            tall(t),
        ],
        out_specs=[tall(t), tall(t)],
        out_shape=[jax.ShapeDtypeStruct((t, d), BF)] * 2,
        compiler_params=pltpu.CompilerParams(vmem_limit_bytes=40 * 2**20),
        name="finish",
    )(upper.astype(jnp.int32)[None], home, back, mix, other)


def after(value, *others):
    return lax.optimization_barrier((value, *others))[0]


def shift_ring(block, by):
    n = 2 * Z
    return lax.ppermute(block, ("z_hi", "z_lo"), [(i, (i + by) % n) for i in range(n)])


def body(act_fwd, act_rev, ids_fwd, ids_rev, probs_fwd, probs_rev, w_gate, w_up, w_down):
    x, z_hi, z_lo = lax.axis_index("x"), lax.axis_index("z_hi"), lax.axis_index("z_lo")
    upper = z_hi == 1
    act_fwd, act_rev = act_fwd[0], act_rev[0]

    def choose(a, b):
        return jnp.where(upper, a, b)

    first = choose(act_rev, act_fwd)
    hop = [((y - 1) % Y * 2 + 1, y * 2 + 1) for y in range(Y)]
    hop += [((y + 1) % Y * 2, y * 2) for y in range(Y)]
    second = lax.ppermute(choose(act_fwd, act_rev), ("y", "z_hi"), hop)

    ids = [choose(ids_fwd[0], ids_rev[0]), choose(ids_rev[0], ids_fwd[0])]
    probs = [choose(probs_fwd[0], probs_rev[0]), choose(probs_rev[0], probs_fwd[0])]
    slots = [slots_of(i) for i in ids]
    mine = jnp.stack(slots)
    slots_all = jnp.stack(
        [mine]
        + [lax.ppermute(mine, "z_lo", [(j, (j + i) % Z) for j in range(Z)]) for i in range(1, Z)]
    )

    swap = [(0, 1), (1, 0)]
    gates, ups, downs = ((w[0], lax.ppermute(w[0], "core", swap)) for w in (w_gate, w_up, w_down))

    low = z_lo < 2
    edge = (z_lo == 0) | (z_lo == Z - 1)
    sources = (
        jnp.where(low, 3, 0),
        jnp.where(low, 2, 1),
        jnp.where(low, 0, 3),
        jnp.where(low, 1, 2),
    )
    row = jnp.arange(X * Z * CAP, dtype=jnp.int32)
    group_of, by_x, far, rank = row // (X * 2 * CAP), row // (2 * CAP) % X, row // CAP % 2, row % CAP
    near_far = [jnp.where(far == 0, sources[i], sources[i + 1]) for i in (0, 2)]
    source = jnp.where(group_of == 0, *near_far)
    order_1 = to_matrix(place(by_x, source, rank))
    order_2 = to_matrix(place(jnp.where(group_of == 0, by_x, (x - by_x) % X), source, rank))
    mixes = [mixing(slots[p], probs[p]) for p in range(2)]
    up, down = [first], [first]

    def at(p, same, k):
        a, b = (up, down) if same else (down, up)
        k = [i + 2 * p for i in k]
        return jnp.where(
            low, jnp.where(edge, a[k[0]], a[k[1]]), jnp.where(edge, b[k[0]], b[k[1]])
        )

    def group(p, same):
        if same:
            return [at(p, True, (1, 2)), at(p, True, (2, 3))]
        return [at(p, False, (4, 3)), at(p, False, (5, 4))]

    def all_x(sent):
        return lax.all_to_all(
            sent.reshape(X, -1, sent.shape[1]), "x", split_axis=0, concat_axis=0, tiled=True
        ).reshape(sent.shape)

    def back(done):
        return lax.all_to_all(
            done.reshape(EXPERTS, CAP, -1), ("x", "z_lo"), split_axis=0, concat_axis=0, tiled=True
        ).reshape(done.shape)

    def home(p):
        return jnp.where(low, down[4 + 2 * p], up[4 + 2 * p])

    def hops(step, *beside):
        above, below = up[-1], down[-1]
        if step == 3:
            above, below = jnp.where(low, above, second), jnp.where(low, second, below)
        ends = (shift_ring(above, 1), shift_ring(below, -1))
        ends, beside = lax.optimization_barrier((ends, beside))
        up.append(ends[0])
        down.append(ends[1])
        return beside

    def picked(parts, p, froms, turn):
        return outgoing(parts, slots_all[:, p], froms, turn, z_lo)

    (gates,) = hops(1, gates)
    (ups,) = hops(2, ups)
    downs, mixes, slots_all = hops(3, downs, mixes, slots_all)
    sent_a = picked(group(0, True), 0, sources[:2], 0)
    hops(4, sent_a)
    got_a = all_x(sent_a)
    order_1, order_2 = hops(5, got_a, order_1, order_2)[1:]
    sent_b = picked(group(0, False), 0, sources[2:], 0)
    gates = hops(6, sent_b, gates)[1]
    got_b = all_x(sent_b)
    done_1 = expert([got_a, got_b], order_1, gates, ups, downs, 10**8)
    hops(7, done_1)
    got_a2 = all_x(after(picked(group(1, True), 1, sources[:2], 0), got_b))
    back_1 = back(after(done_1, got_a2))
    got_b2 = over_x(picked(group(1, False), 1, sources[2:], x))
    done_2 = expert([got_a2, *got_b2], order_2, gates, ups, downs, 2 * 10**11)
    out_1 = combine(home(0), after(back_1, done_2), mixes[0])
    out_a, out_b = finish(upper, home(1), back(done_2), mixes[1], out_1)
    return out_a[None], out_b[None]


def solution(mesh):
    split = Mesh(mesh.devices.reshape(Y, 2, X, Z, 2), ("y", "z_hi", "x", "z_lo", "core"))
    section, spread = ("y", "z_hi"), ("x", "z_lo", "core")
    tokens = P(section, spread, None)
    return jax.shard_map(
        body,
        mesh=split,
        in_specs=(tokens,) * 6 + (P(section, None, spread),) * 2 + (tokens,),
        out_specs=(tokens, tokens),
        check_vma=False,
    )
```

```python
import jax
import jax.numpy as jnp
from jax import lax
from jax.experimental import pallas as pl
from jax.experimental.pallas import tpu as pltpu
from jax.sharding import Mesh
from jax.sharding import PartitionSpec as P

EXPERTS = 16
CAP = 24
X, Z, Y = 4, 4, 4
BF = jnp.bfloat16
F32 = jnp.float32


def slots_of(ids):
    flat = ids.reshape(-1)
    n = flat.shape[0]
    one_hot = (flat[:, None] == jnp.arange(EXPERTS, dtype=jnp.int32)[None, :]).astype(BF)
    place = jnp.arange(n, dtype=jnp.int32)
    below = (place[:, None] > place[None, :]).astype(BF)
    counts = jnp.dot(below, one_hot, preferred_element_type=F32)
    rank = jnp.sum(counts * one_hot.astype(F32), axis=1).astype(jnp.int32)
    return (flat * CAP + rank).reshape(ids.shape)


def outgoing(parts, slots, sources, turn, z_lo):
    t, n = parts[0].shape[0], len(parts)
    row = jnp.arange(X * n * CAP, dtype=jnp.int32)
    block, which, rank = row // (n * CAP), row // CAP % n, row % CAP
    target = ((turn + block) % X * Z + z_lo) * CAP + rank
    held = jnp.arange(n * t, dtype=jnp.int32) // t
    flat = jnp.concatenate([lax.dynamic_index_in_dim(slots, (z_lo - s) % Z, 0, False) for s in sources], axis=0)
    hit = (flat[None, :, 0] == target[:, None]) | (flat[None, :, 1] == target[:, None])
    pick = (hit & (held[None, :] == which[:, None])).astype(BF)
    return jnp.dot(pick, jnp.concatenate(parts, axis=0), preferred_element_type=F32).astype(BF)


def over_x(sent):
    n = sent.shape[0] // X
    blocks = [sent[i * n : (i + 1) * n] for i in range(X)]
    moved = [lax.ppermute(blocks[i], "x", [(j, (j + i) % X) for j in range(X)]) for i in range(1, X)]
    return [blocks[0], *moved]


def place(from_x, source, rank):
    return (from_x * Z + source) * CAP + rank


def to_matrix(to):
    row = jnp.arange(to.shape[0], dtype=jnp.int32)
    return (row[:, None] == to[None, :]).astype(BF)


STEPS = 4


def expert_kernel(n_parts, *refs):
    parts, (order, g0, g1, u0, u1, d0, d1, out, gate, up, hidden) = refs[:n_parts], refs[n_parts:]
    step = pl.program_id(0)

    @pl.when(step == 0)
    def _():
        gate[...] = jnp.zeros_like(gate)
        up[...] = jnp.zeros_like(up)

    @pl.when(step < STEPS)
    def _():
        rows = jnp.concatenate([p[...] for p in parts], axis=0)
        gate[...] += jnp.dot(rows, jnp.concatenate([g0[...], g1[...]], axis=1), preferred_element_type=F32)
        up[...] += jnp.dot(rows, jnp.concatenate([u0[...], u1[...]], axis=1), preferred_element_type=F32)

    @pl.when(step == STEPS - 1)
    def _():
        pre = gate[...]
        value = (pre / (1.0 + jnp.exp(-pre)) * up[...]).astype(BF)
        hidden[...] = jnp.dot(order[...], value, preferred_element_type=F32).astype(BF)

    @pl.when(step >= STEPS)
    def _():
        down = jnp.concatenate([d0[...], d1[...]], axis=0)
        out[...] = jnp.dot(hidden[...], down, preferred_element_type=F32).astype(BF)


def expert(parts, order, gates, ups, downs, flops):
    n, d = order.shape[0], parts[0].shape[1]
    half = gates[0].shape[1]
    cols = d // STEPS

    def first(i):
        return jnp.minimum(i, STEPS - 1)

    def second(i):
        return jnp.maximum(i - STEPS, 0)

    in_specs = [pl.BlockSpec((p.shape[0], cols), lambda i: (0, first(i))) for p in parts]
    in_specs += [pl.BlockSpec((n, n), lambda i: (0, 0))]
    in_specs += [pl.BlockSpec((cols, half), lambda i: (first(i), 0))] * 4
    in_specs += [pl.BlockSpec((half, cols), lambda i: (0, second(i)))] * 2
    return pl.pallas_call(
        lambda *refs: expert_kernel(len(parts), *refs),
        grid=(2 * STEPS,),
        in_specs=in_specs,
        out_specs=pl.BlockSpec((n, cols), lambda i: (0, second(i))),
        out_shape=jax.ShapeDtypeStruct((n, d), BF),
        scratch_shapes=[
            pltpu.VMEM((n, 2 * half), F32),
            pltpu.VMEM((n, 2 * half), F32),
            pltpu.VMEM((n, 2 * half), BF),
        ],
        compiler_params=pltpu.CompilerParams(vmem_limit_bytes=58 * 2**20),
        cost_estimate=pl.CostEstimate(flops=flops, bytes_accessed=10**6, transcendentals=0),
        name="expert",
    )(*parts, order, *gates, *ups, *downs)


def mixing(slots, probs):
    gates = probs / jnp.sum(probs, axis=1, keepdims=True)
    spot = jnp.arange(EXPERTS * CAP, dtype=jnp.int32)
    mix = jnp.sum(
        jnp.where(slots[:, :, None] == spot[None, None, :], gates[:, :, None], 0.0), axis=1
    )
    high = lax.reduce_precision(mix, 8, 7)
    return jnp.concatenate([high, mix - high], axis=0).astype(BF)


def combine(home, back, mix):
    summed = jnp.dot(mix, back, preferred_element_type=F32)
    t = home.shape[0]
    return (home.astype(F32) + (summed[:t] + summed[t:])).astype(BF)


def finish_kernel(upper, home, back, mix, other, out_a, out_b):
    last = combine(home[...], back[...], mix[...])
    swap = upper[0] == 1
    out_a[...] = jnp.where(swap, other[...], last)
    out_b[...] = jnp.where(swap, last, other[...])


def finish(upper, home, back, mix, other):
    t, d = home.shape
    cols = 1024

    def tall(rows):
        return pl.BlockSpec((rows, cols), lambda i: (0, i))

    return pl.pallas_call(
        finish_kernel,
        grid=(d // cols,),
        in_specs=[
            pl.BlockSpec(memory_space=pltpu.SMEM),
            tall(t),
            tall(back.shape[0]),
            pl.BlockSpec(mix.shape, lambda i: (0, 0)),
            tall(t),
        ],
        out_specs=[tall(t), tall(t)],
        out_shape=[jax.ShapeDtypeStruct((t, d), BF)] * 2,
        compiler_params=pltpu.CompilerParams(vmem_limit_bytes=40 * 2**20),
        name="finish",
    )(upper.astype(jnp.int32)[None], home, back, mix, other)


def after(value, *others):
    return lax.optimization_barrier((value, *others))[0]


def shift_ring(block, by):
    n = 2 * Z
    return lax.ppermute(block, ("z_hi", "z_lo"), [(i, (i + by) % n) for i in range(n)])


def body(act_fwd, act_rev, ids_fwd, ids_rev, probs_fwd, probs_rev, w_gate, w_up, w_down):
    x, z_hi, z_lo = lax.axis_index("x"), lax.axis_index("z_hi"), lax.axis_index("z_lo")
    upper = z_hi == 1
    act_fwd, act_rev = act_fwd[0], act_rev[0]

    def choose(a, b):
        return jnp.where(upper, a, b)

    first = choose(act_rev, act_fwd)
    hop = [((y - 1) % Y * 2 + 1, y * 2 + 1) for y in range(Y)]
    hop += [((y + 1) % Y * 2, y * 2) for y in range(Y)]
    second = lax.ppermute(choose(after(act_fwd, first), act_rev), ("y", "z_hi"), hop)

    ids = [choose(ids_fwd[0], ids_rev[0]), choose(ids_rev[0], ids_fwd[0])]
    probs = [choose(probs_fwd[0], probs_rev[0]), choose(probs_rev[0], probs_fwd[0])]
    slots = [slots_of(i) for i in ids]
    mine = jnp.stack(slots)
    slots_all = jnp.stack(
        [mine]
        + [lax.ppermute(mine, "z_lo", [(j, (j + i) % Z) for j in range(Z)]) for i in range(1, Z)]
    )

    swap = [(0, 1), (1, 0)]
    gates, ups, downs = ((w[0], lax.ppermute(w[0], "core", swap)) for w in (w_gate, w_up, w_down))

    low = z_lo < 2
    edge = (z_lo == 0) | (z_lo == Z - 1)
    sources = (
        jnp.where(low, 3, 0),
        jnp.where(low, 2, 1),
        jnp.where(low, 0, 3),
        jnp.where(low, 1, 2),
    )
    row = jnp.arange(X * Z * CAP, dtype=jnp.int32)
    group_of, by_x, far, rank = row // (X * 2 * CAP), row // (2 * CAP) % X, row // CAP % 2, row % CAP
    near_far = [jnp.where(far == 0, sources[i], sources[i + 1]) for i in (0, 2)]
    source = jnp.where(group_of == 0, *near_far)
    order_1 = to_matrix(place(by_x, source, rank))
    order_2 = to_matrix(place(jnp.where(group_of == 0, by_x, (x - by_x) % X), source, rank))
    mixes = [mixing(slots[p], probs[p]) for p in range(2)]
    up, down = [first], [first]

    def at(p, same, k):
        a, b = (up, down) if same else (down, up)
        k = [i + 2 * p for i in k]
        return jnp.where(
            low, jnp.where(edge, a[k[0]], a[k[1]]), jnp.where(edge, b[k[0]], b[k[1]])
        )

    def group(p, same):
        if same:
            return [at(p, True, (1, 2)), at(p, True, (2, 3))]
        return [at(p, False, (4, 3)), at(p, False, (5, 4))]

    def all_x(sent):
        return lax.all_to_all(
            sent.reshape(X, -1, sent.shape[1]), "x", split_axis=0, concat_axis=0, tiled=True
        ).reshape(sent.shape)

    def back(done):
        return lax.all_to_all(
            done.reshape(EXPERTS, CAP, -1), ("x", "z_lo"), split_axis=0, concat_axis=0, tiled=True
        ).reshape(done.shape)

    def home(p):
        return jnp.where(low, down[4 + 2 * p], up[4 + 2 * p])

    def hops(step, *beside):
        above, below = up[-1], down[-1]
        if step == 3:
            above, below = jnp.where(low, above, second), jnp.where(low, second, below)
        ends = (shift_ring(above, 1), shift_ring(below, -1))
        ends, beside = lax.optimization_barrier((ends, beside))
        up.append(ends[0])
        down.append(ends[1])
        return beside

    def picked(parts, p, froms, turn):
        return outgoing(parts, slots_all[:, p], froms, turn, z_lo)

    (gates,) = hops(1, gates)
    (ups,) = hops(2, ups)
    downs, mixes, slots_all = hops(3, downs, mixes, slots_all)
    sent_a = picked(group(0, True), 0, sources[:2], 0)
    hops(4, sent_a)
    got_a = all_x(sent_a)
    order_1, order_2 = hops(5, got_a, order_1, order_2)[1:]
    sent_b = picked(group(0, False), 0, sources[2:], 0)
    gates = hops(6, sent_b, gates)[1]
    got_b = all_x(sent_b)
    done_1 = expert([got_a, got_b], order_1, gates, ups, downs, 10**8)
    hops(7, done_1)
    got_a2 = all_x(after(picked(group(1, True), 1, sources[:2], 0), got_b))
    back_1 = back(after(done_1, got_a2))
    got_b2 = over_x(picked(group(1, False), 1, sources[2:], x))
    done_2 = expert([got_a2, *got_b2], order_2, gates, ups, downs, 48 * 10**9)
    out_1 = combine(home(0), after(back_1, done_2), mixes[0])
    out_a, out_b = finish(upper, home(1), back(done_2), mixes[1], out_1)
    return out_a[None], out_b[None]


def solution(mesh):
    split = Mesh(mesh.devices.reshape(Y, 2, X, Z, 2), ("y", "z_hi", "x", "z_lo", "core"))
    section, spread = ("y", "z_hi"), ("x", "z_lo", "core")
    tokens = P(section, spread, None)
    return jax.shard_map(
        body,
        mesh=split,
        in_specs=(tokens,) * 6 + (P(section, None, spread),) * 2 + (tokens,),
        out_specs=(tokens, tokens),
        check_vma=False,
    )
```
